32 devices in a mesh: seq: 16 (over z, x, core), tp: 2 (over y).
Axes of the slice: x: 2, y: 2, z: 4, core: 2. Of those that a mesh axis runs over, the one named last changes fastest.
Arguments:
- tokens: bfloat16 [2048, 2560], P('seq', 'tp'), may hold values from -6 to 6
- seg_ids: int32 [2048], P('seq'), may hold values from 0 to 3, never falling along the last dimension, each value on 1 to 1024 neighbouring positions
- norm_gain: bfloat16 [2560], replicated, may hold values from 0.099609375 to 1.8984375
- w_query: bfloat16 [2560, 2048], P('seq', 'tp'), may hold values from -3 to 3
- w_keyval: bfloat16 [2560, 512], P('seq'), may hold values from -1 to 1
- w_out: bfloat16 [2048, 2560], P('tp', 'seq'), may hold values from -0.125 to 0.125
Outputs:
- hidden: bfloat16 [2048, 2560], P('seq', 'tp')
- kv_cache: bfloat16 [2048, 512], P('seq')
The draws below stay inside these ranges and needn't reach their ends.
Inputs may be any that keep to these rules, and one draw needn't show every extreme that they name: `seg_ids`: ids never fall along the stream; each of the 4 requests holds 1 to 1024 consecutive tokens, one exactly 1024.
All inputs are finite; a program needn't handle non-finite values.
Results may differ from the reference program's by a relative error of at most 0.0085.
Values may be sent and summed in bfloat16 or wider, within the bound.
A program may use at most 64 MiB of HBM per device.

```python
import math
import jax
import jax.numpy as jnp
import numpy as np
from jax import lax

D = 2560
HEADS = 8
HD = 256
WINDOW = 2048
TOK_DEV = 128
TOKENS = 2048
SEGS = 4
MOST = 1024
N_TP = 2


def weight_pair(key):
    base = jax.random.fold_in(key, 7)
    key_kv = jax.random.fold_in(base, 1)
    key_query = jax.random.fold_in(base, 2)
    scale = D ** (-0.5)
    keyval = jnp.clip(jax.random.normal(key_kv, (D, 2 * HD), jnp.float32), -6.0, 6.0) * scale
    query = jnp.clip(jax.random.normal(key_query, (D, HEADS * HD), jnp.float32), -6.0, 6.0) * scale
    return (query, keyval)


def draw_w_query(key, part):
    return weight_pair(key)[0].astype(jnp.bfloat16)


def draw_w_keyval(key, part):
    return weight_pair(key)[1].astype(jnp.bfloat16)


def draw_tokens(key, part):
    values = jnp.clip(jax.random.normal(key, (TOKENS, D), jnp.float32), -6.0, 6.0)
    return values.astype(jnp.bfloat16)


def levels(stream_key, extent, cuts, least, top_value):
    level, own = 1.0, jax.random.fold_in(stream_key, 6)
    for position, shards_of in cuts:
        heights = jnp.exp(jax.random.uniform(jax.random.fold_in(own, position), (shards_of,), jnp.float32, least / len(cuts), top_value / len(cuts)))
        level = level * jnp.repeat(heights, extent[position] // shards_of).reshape([-1 if axis == position else 1 for axis in range(len(extent))])
    return level


def length_profile(amount, total, most, skew):
    weights = [(1 << 20) // math.isqrt(rank ** skew) + 1 for rank in range(2, amount + 1)]
    surplus, holding = total - most - (amount - 1), [1] * (amount - 1)
    while surplus > 0:
        free = [i for i in range(amount - 1) if holding[i] < most]
        whole, left = sum([weights[i] for i in free]), surplus
        for i in free:
            more = min(most - holding[i], max(1, left * weights[i] // whole), surplus)
            holding[i] = holding[i] + more
            surplus = surplus - more
    return np.array([most] + holding)


def uneven(key, count, total, bound, skew):
    if count == 2:
        one = jax.random.randint(key, (), max(1, total - bound), min(bound, total - 1) + 1)
        return jnp.stack([one, total - one])
    lengths = jnp.asarray(length_profile(count, total, bound, skew), jnp.int32)
    couples = (count - 1) // 2
    source_of, receiver = lengths[1:1 + 2 * couples:2], lengths[2:2 + 2 * couples:2]
    margin = jnp.minimum(source_of - 1, bound - receiver)
    moved = jax.random.randint(jax.random.fold_in(key, 1), (couples,), 0, 1 << 20) % (margin + 1)
    lengths = lengths.at[1:1 + 2 * couples:2].set(source_of - moved).at[2:2 + 2 * couples:2].set(receiver + moved)
    return lengths[jax.random.permutation(jax.random.fold_in(key, 2), count)]


def centred(rng, extent, scale, bound, shards=(), kind=jnp.bfloat16):
    entries = scale * jax.random.normal(rng, extent, jnp.float32)
    if shards:
        entries = entries * levels(rng, extent, shards, -0.22, 0.18)
    return jnp.clip(entries, -bound, bound).astype(kind)


def setup_inputs(seed: int = 0) -> dict:
    seeds = jax.random.split(jax.random.key(seed), 7)
    return {
        "tokens": draw_tokens(jax.random.fold_in(seeds[6], 71), 0),
        "seg_ids": jnp.searchsorted(jnp.cumsum(uneven(seeds[1], SEGS, TOKENS, MOST, 2)), jnp.arange(TOKENS), side="right").astype(jnp.int32),
        "norm_gain": jnp.clip(1.0 + 0.18 * jax.random.normal(seeds[2], (D,), jnp.float32), 0.099609375, 1.8984375).astype(jnp.bfloat16),
        "w_query": draw_w_query(jax.random.fold_in(seeds[6], 71), 0),
        "w_keyval": draw_w_keyval(jax.random.fold_in(seeds[6], 71), 0),
        "w_out": centred(seeds[5], (HEADS * HD, D), (HEADS * HD) ** -0.5, 0.125, ((0, 2), (1, 16))),
    }


def rms_norm(values, gain):
    wide = values.astype(jnp.float32)
    scaled = wide * lax.rsqrt(lax.optimization_barrier(jnp.mean(wide * wide, axis=-1, keepdims=True)) + 1e-06)
    return (scaled * gain.astype(jnp.float32)).astype(jnp.bfloat16)

def rotate(tensor, positions):
    quarter = tensor.shape[-1] // 4
    freq = 10000.0 ** (-jnp.arange(quarter, dtype=jnp.float32) / quarter)
    angle = positions[:, None, None] * freq
    cosine = jnp.cos(angle)
    sine = jnp.sin(angle)
    first = tensor[..., :quarter]
    second = tensor[..., quarter:2 * quarter]
    return jnp.concatenate([first * cosine - second * sine, second * cosine + first * sine, tensor[..., 2 * quarter:]], axis=-1)

def reference(tokens, seg_ids, norm_gain, w_query, w_keyval, w_out):
    normed = rms_norm(tokens, norm_gain)
    labels = jnp.arange(SEGS, dtype=jnp.int32)
    starts = lax.optimization_barrier(jnp.sum((seg_ids[None, :] < labels[:, None]).astype(jnp.int32), axis=1))
    token_index = jnp.arange(TOKENS, dtype=jnp.int32)
    own_start = jnp.take(starts, seg_ids)
    positions = (token_index - own_start).astype(jnp.float32)
    query_raw = jnp.dot(normed, w_query, preferred_element_type=jnp.float32)
    keyval_raw = jnp.dot(normed, w_keyval, preferred_element_type=jnp.float32)
    queries = rotate(query_raw.reshape(TOKENS, HEADS, HD), positions).astype(jnp.bfloat16)
    key_rows = rotate(keyval_raw[:, None, :HD], positions)[:, 0, :]
    kv_cache = jnp.concatenate([key_rows, keyval_raw[:, HD:]], axis=1).astype(jnp.bfloat16)
    pad_kv = jnp.concatenate([jnp.zeros((WINDOW, 2 * HD), jnp.bfloat16), kv_cache], axis=0)
    pad_seg = jnp.concatenate([jnp.full((WINDOW,), -1, jnp.int32), seg_ids], axis=0)

    def attend(block_idx):
        begin_at = (block_idx * TOK_DEV).astype(jnp.int32)
        q_block = lax.dynamic_slice_in_dim(queries, begin_at, TOK_DEV, 0).astype(jnp.float32)
        kv_block = lax.dynamic_slice_in_dim(pad_kv, begin_at, TOK_DEV + WINDOW, 0)
        seg_block = lax.dynamic_slice_in_dim(pad_seg, begin_at, TOK_DEV + WINDOW, 0)
        q_seg = lax.dynamic_slice_in_dim(seg_ids, begin_at, TOK_DEV, 0)
        q_index = begin_at + jnp.arange(TOK_DEV, dtype=jnp.int32)
        k_index = begin_at - WINDOW + jnp.arange(TOK_DEV + WINDOW, dtype=jnp.int32)
        live = (seg_block[None, :] == q_seg[:, None]) & (k_index[None, :] <= q_index[:, None]) & (q_index[:, None] - k_index[None, :] < WINDOW)
        scores = jnp.einsum('qhd,kd->hqk', q_block, kv_block[:, :HD].astype(jnp.float32)) * HD ** (-0.5)
        scores = jnp.where(live[None], scores, -1e+30)
        peak = lax.optimization_barrier(jnp.max(scores, axis=2, keepdims=True))
        powered = jnp.exp(scores - peak)
        weights = (powered / lax.optimization_barrier(jnp.sum(powered, axis=2, keepdims=True))).astype(jnp.bfloat16)
        result = jnp.einsum('hqk,kd->qhd', weights.astype(jnp.float32), kv_block[:, HD:].astype(jnp.float32)).astype(jnp.bfloat16)
        return result.reshape(TOK_DEV, HEADS * HD)
    attended = lax.map(attend, jnp.arange(TOKENS // TOK_DEV, dtype=jnp.int32)).reshape(TOKENS, HEADS * HD)
    group = HEADS * HD // N_TP
    summed = jnp.zeros((TOKENS, D), jnp.float32)
    for group_idx in range(N_TP):
        partial_value = jnp.dot(attended[:, group_idx * group:(group_idx + 1) * group], w_out[group_idx * group:(group_idx + 1) * group], preferred_element_type=jnp.float32).astype(jnp.bfloat16)
        summed = summed + partial_value.astype(jnp.float32)
    hidden = (tokens.astype(jnp.float32) + summed).astype(jnp.bfloat16)
    return (hidden, kv_cache)
```

```python
import jax
import jax.numpy as jnp
from jax import lax
from jax.sharding import PartitionSpec as P

HD = 256
WINDOW = 2048
SEG_MEAN = 512


def from_behind(x, axis, by):
    devices = lax.axis_size(axis)
    pairs = [(i, i + by) for i in range(devices) if 0 <= i + by < devices]
    return lax.ppermute(x, axis, pairs)


def rms_norm(values, gain):
    wide = values.astype(jnp.float32)
    scaled = wide * lax.rsqrt(jnp.mean(wide * wide, axis=-1, keepdims=True) + 1e-06)
    return (scaled * gain.astype(jnp.float32)).astype(jnp.bfloat16)


def rotate(tensor, positions):
    quarter = tensor.shape[-1] // 4
    freq = 10000.0 ** (-jnp.arange(quarter, dtype=jnp.float32) / quarter)
    angle = positions[:, None, None] * freq
    cosine = jnp.cos(angle)
    sine = jnp.sin(angle)
    first = tensor[..., :quarter]
    second = tensor[..., quarter : 2 * quarter]
    return jnp.concatenate(
        [
            first * cosine - second * sine,
            second * cosine + first * sine,
            tensor[..., 2 * quarter :],
        ],
        axis=-1,
    )


def per_device(tokens, seg_ids, norm_gain, w_query, w_keyval, w_out):
    tok_rows = tokens.shape[0]
    seq_count = lax.axis_size("seq")
    my_index = lax.axis_index("seq")
    gathered = lax.all_gather(tokens, "tp", axis=1, tiled=True)
    normed = rms_norm(gathered, norm_gain)
    seg_total = tok_rows * seq_count // SEG_MEAN
    labels = jnp.arange(seg_total, dtype=jnp.int32)
    below = jnp.sum((seg_ids[None, :] < labels[:, None]).astype(jnp.int32), axis=1)
    starts = lax.psum(below, "seq")
    own_start = jnp.sum(jnp.where(seg_ids[:, None] == labels[None, :], starts[None, :], 0), axis=1)
    token_index = my_index * tok_rows + jnp.arange(tok_rows, dtype=jnp.int32)
    positions = (token_index - own_start).astype(jnp.float32)
    query_raw = jnp.dot(
        normed,
        lax.all_gather(w_query, "seq", axis=0, tiled=True),
        preferred_element_type=jnp.float32,
    )
    keyval_raw = jnp.dot(
        normed,
        lax.all_gather(w_keyval, "seq", axis=0, tiled=True),
        preferred_element_type=jnp.float32,
    )
    local_heads = w_query.shape[1] // HD
    queries = rotate(query_raw.reshape(tok_rows, local_heads, HD), positions).astype(jnp.bfloat16)
    key_rows = rotate(keyval_raw[:, None, :HD], positions)[:, 0, :]
    kv_cache = jnp.concatenate([key_rows, keyval_raw[:, HD:]], axis=1).astype(jnp.bfloat16)
    reach = min(WINDOW // tok_rows, seq_count - 1)

    def advance(counter, state):
        current, current_seg, store, store_seg = state
        current, current_seg = from_behind((current, current_seg), "seq", 1)
        slot = reach - 1 - counter
        store = lax.dynamic_update_slice_in_dim(store, current[None], slot, 0)
        store_seg = lax.dynamic_update_slice_in_dim(store_seg, current_seg[None], slot, 0)
        return (current, current_seg, store, store_seg)

    if reach == seq_count - 1:
        block_kv = lax.all_gather(kv_cache, "seq", axis=0, tiled=True)
        block_seg = lax.all_gather(seg_ids, "seq", axis=0, tiled=True)
        first_key = 0
    else:
        store_init = jnp.zeros((reach, tok_rows, kv_cache.shape[1]), jnp.bfloat16)
        seg_init = jnp.zeros((reach, tok_rows), jnp.int32)
        final_state = lax.fori_loop(0, reach, advance, (kv_cache, seg_ids, store_init, seg_init))
        block_kv = jnp.concatenate(
            [final_state[2].reshape(reach * tok_rows, kv_cache.shape[1]), kv_cache], axis=0
        )
        block_seg = jnp.concatenate([final_state[3].reshape(reach * tok_rows), seg_ids], axis=0)
        first_key = (my_index - reach) * tok_rows
    key_index = first_key + jnp.arange((reach + 1) * tok_rows, dtype=jnp.int32)
    live = (block_seg[None, :] == seg_ids[:, None]) & (key_index[None, :] <= token_index[:, None])
    live = live & (token_index[:, None] - key_index[None, :] < WINDOW) & (key_index[None, :] >= 0)
    all_keys = block_kv[:, :HD]
    all_values = block_kv[:, HD:]
    head_outputs = []
    for head_idx in range(local_heads):
        scores = lax.dot_general(
            queries[:, head_idx, :],
            all_keys,
            (((1,), (1,)), ((), ())),
            preferred_element_type=jnp.float32,
        ) * HD ** (-0.5)
        scores = jnp.where(live, scores, -1e30)
        peak = jnp.max(scores, axis=1, keepdims=True)
        powered = jnp.exp(scores - peak)
        weights = (powered / jnp.sum(powered, axis=1, keepdims=True)).astype(jnp.bfloat16)
        head_outputs.append(
            jnp.dot(weights, all_values, preferred_element_type=jnp.float32).astype(jnp.bfloat16)
        )
    attended = jnp.concatenate(head_outputs, axis=1)
    partial_value = jnp.dot(
        attended,
        lax.all_gather(w_out, "seq", axis=1, tiled=True),
        preferred_element_type=jnp.float32,
    )
    summed = lax.psum_scatter(
        partial_value.astype(jnp.bfloat16), "tp", scatter_dimension=1, tiled=True
    ).astype(jnp.float32)
    hidden = (tokens.astype(jnp.float32) + summed).astype(jnp.bfloat16)
    return (hidden, kv_cache)


def solution(mesh):
    in_specs = (P("seq", "tp"), P("seq"), P(), P("seq", "tp"), P("seq", None), P("tp", "seq"))
    out_specs = (P("seq", "tp"), P("seq", None))
    return jax.shard_map(
        per_device, mesh=mesh, in_specs=in_specs, out_specs=out_specs, check_vma=False
    )
```

```python
import jax
import jax.numpy as jnp
from jax import lax
from jax.experimental import pallas as pl
from jax.experimental.pallas import tpu as pltpu
from jax.sharding import PartitionSpec as P

HD = 256
WINDOW = 2048
SEG_MEAN = 512
CHUNK = 32


def from_behind(x, axis, by):
    devices = lax.axis_size(axis)
    pairs = [(i, i + by) for i in range(devices) if 0 <= i + by < devices]
    return lax.ppermute(x, axis, pairs)


def rms_norm(values, gain):
    wide = values.astype(jnp.float32)
    scaled = wide * lax.rsqrt(jnp.mean(wide * wide, axis=-1, keepdims=True) + 1e-06)
    return (scaled * gain.astype(jnp.float32)).astype(jnp.bfloat16)


def rotate(tensor, positions):
    quarter = tensor.shape[-1] // 4
    freq = 10000.0 ** (-jnp.arange(quarter, dtype=jnp.float32) / quarter)
    angle = positions[:, None, None] * freq
    cosine = jnp.cos(angle)
    sine = jnp.sin(angle)
    first = tensor[..., :quarter]
    second = tensor[..., quarter : 2 * quarter]
    return jnp.concatenate(
        [
            first * cosine - second * sine,
            second * cosine + first * sine,
            tensor[..., 2 * quarter :],
        ],
        axis=-1,
    )


def per_device(tokens, seg_ids, norm_gain, w_query, w_keyval, w_out):
    tok_rows = tokens.shape[0]
    seq_count = lax.axis_size("seq")
    my_index = lax.axis_index("seq")
    gathered = lax.all_gather(tokens, "tp", axis=1, tiled=True)
    normed = rms_norm(gathered, norm_gain)
    seg_total = tok_rows * seq_count // SEG_MEAN
    labels = jnp.arange(seg_total, dtype=jnp.int32)
    below = jnp.sum((seg_ids[None, :] < labels[:, None]).astype(jnp.int32), axis=1)
    starts = lax.psum(below, "seq")
    own_start = jnp.sum(jnp.where(seg_ids[:, None] == labels[None, :], starts[None, :], 0), axis=1)
    token_index = my_index * tok_rows + jnp.arange(tok_rows, dtype=jnp.int32)
    positions = (token_index - own_start).astype(jnp.float32)
    query_raw = jnp.dot(
        normed,
        lax.all_gather(w_query, "seq", axis=0, tiled=True),
        preferred_element_type=jnp.float32,
    )
    keyval_raw = jnp.dot(
        normed,
        lax.all_gather(w_keyval, "seq", axis=0, tiled=True),
        preferred_element_type=jnp.float32,
    )
    local_heads = w_query.shape[1] // HD
    queries = rotate(query_raw.reshape(tok_rows, local_heads, HD), positions).astype(jnp.bfloat16)
    key_rows = rotate(keyval_raw[:, None, :HD], positions)[:, 0, :]
    kv_cache = jnp.concatenate([key_rows, keyval_raw[:, HD:]], axis=1).astype(jnp.bfloat16)
    reach = min(WINDOW // tok_rows, seq_count - 1)

    def advance(counter, state):
        current, current_seg, store, store_seg = state
        current, current_seg = from_behind((current, current_seg), "seq", 1)
        slot = reach - 1 - counter
        store = lax.dynamic_update_slice_in_dim(store, current[None], slot, 0)
        store_seg = lax.dynamic_update_slice_in_dim(store_seg, current_seg[None], slot, 0)
        return (current, current_seg, store, store_seg)

    if reach == seq_count - 1:
        block_kv = lax.all_gather(kv_cache, "seq", axis=0, tiled=True)
        block_seg = lax.all_gather(seg_ids, "seq", axis=0, tiled=True)
        first_key = 0
    else:
        store_init = jnp.zeros((reach, tok_rows, kv_cache.shape[1]), jnp.bfloat16)
        seg_init = jnp.zeros((reach, tok_rows), jnp.int32)
        final_state = lax.fori_loop(0, reach, advance, (kv_cache, seg_ids, store_init, seg_init))
        block_kv = jnp.concatenate(
            [final_state[2].reshape(reach * tok_rows, kv_cache.shape[1]), kv_cache], axis=0
        )
        block_seg = jnp.concatenate([final_state[3].reshape(reach * tok_rows), seg_ids], axis=0)
        first_key = (my_index - reach) * tok_rows
    key_index = first_key + jnp.arange((reach + 1) * tok_rows, dtype=jnp.int32)
    live = (block_seg[None, :] == seg_ids[:, None]) & (key_index[None, :] <= token_index[:, None])
    live = live & (token_index[:, None] - key_index[None, :] < WINDOW) & (key_index[None, :] >= 0)
    all_keys = block_kv[:, :HD]
    all_values = block_kv[:, HD:]
    head_outputs = []
    for head_idx in range(local_heads):
        scores = lax.dot_general(
            queries[:, head_idx, :],
            all_keys,
            (((1,), (1,)), ((), ())),
            preferred_element_type=jnp.float32,
        ) * HD ** (-0.5)
        scores = jnp.where(live, scores, -1e30)
        peak = jnp.max(scores, axis=1, keepdims=True)
        powered = jnp.exp(scores - peak)
        weights = (powered / jnp.sum(powered, axis=1, keepdims=True)).astype(jnp.bfloat16)
        head_outputs.append(
            jnp.dot(weights, all_values, preferred_element_type=jnp.float32).astype(jnp.bfloat16)
        )
    attended = jnp.concatenate(head_outputs, axis=1)
    partial_value = jnp.dot(
        attended,
        lax.all_gather(w_out, "seq", axis=1, tiled=True),
        preferred_element_type=jnp.float32,
    )
    summed = lax.psum_scatter(
        partial_value.astype(jnp.bfloat16), "tp", scatter_dimension=1, tiled=True
    ).astype(jnp.float32)
    hidden = (tokens.astype(jnp.float32) + summed).astype(jnp.bfloat16)
    return (hidden, kv_cache)


MESH = pl.DeviceIdType.MESH


def block_kernel(
    tok_ref, seg_ref, segcol_ref, gain_ref, freq_ref, wq_ref, wkv_ref, wo_ref,
    hidden_ref, cache_ref,
    tok, normed, seg, wkv, wq, wo, kv, half, queries, attended, partial, other,
    local_sem, send_sem, recv_sem, pair_send, pair_recv,
):
    me = lax.axis_index("seq")
    tp = lax.axis_index("tp")
    z, x, c = me // 4, lax.rem(me // 2, 2), lax.rem(me, 2)
    rows = tok_ref.shape[0]
    width = tok_ref.shape[1]
    shard = wq_ref.shape[0]
    count = wq_ref.shape[1]
    heads = count // HD
    total = rows * 16

    def index(zz, xx, cc):
        return (zz * 2 + xx) * 2 + cc

    z_peers = [index(lax.rem(z + k, 4), x, c) for k in (1, 2, 3)]
    x_peer = index(z, 1 - x, c)
    c_peer = index(z, x, 1 - c)

    barrier = pltpu.get_barrier_semaphore()
    for peer in z_peers + [x_peer, c_peer]:
        pl.semaphore_signal(barrier, inc=1, device_id=(peer, tp), device_id_type=MESH)
    pl.semaphore_signal(barrier, inc=1, device_id=(me, 1 - tp), device_id_type=MESH)

    mine = [
        pltpu.make_async_copy(wq_ref, wq.at[pl.ds(pl.multiple_of(me * shard, shard), shard)], local_sem.at[0]),
        pltpu.make_async_copy(wo_ref, wo.at[pl.ds(pl.multiple_of(me * shard, shard), shard)], local_sem.at[1]),
    ]
    for copy in mine:
        copy.start()
    wkv[pl.ds(pl.multiple_of(me * shard, shard), shard), :] = jnp.where(
        tp == 0, wkv_ref[:, :HD], wkv_ref[:, HD:]
    )
    seg[me] = seg_ref[...]
    pl.semaphore_wait(barrier, 6)

    def pair(which, src, dst):
        return pltpu.make_async_remote_copy(
            src_ref=src, dst_ref=dst, send_sem=pair_send.at[which], recv_sem=pair_recv.at[which],
            device_id=(me, 1 - tp), device_id_type=MESH,
        )

    tok_copy = pair(0, tok_ref, tok.at[tp])
    tok_copy.start()
    tok[pl.ds(tp, 1)] = tok_ref[...][None]

    steps = [(seg, 0, 0, 0), (wkv, shard, 0, shard)]
    steps += [(wq, shard, at, CHUNK) for at in range(0, shard, CHUNK)]
    steps += [(wo, shard, at, CHUNK) for at in range(0, shard, CHUNK)]
    steps += [(kv, rows, 0, rows)]
    per = shard // CHUNK
    Q0, O0, KV = 2, 2 + per, 2 + 2 * per
    sends = []

    def view(s, slot):
        buffer, each, at, size = steps[s]
        if each == 0:
            return buffer.at[slot]
        return buffer.at[pl.ds(pl.multiple_of(slot * each + at, 16), size)]

    def copy_of(s, slot, which, peer, src=None):
        return pltpu.make_async_remote_copy(
            src_ref=view(s, slot) if src is None else src, dst_ref=view(s, slot),
            send_sem=send_sem.at[s, which], recv_sem=recv_sem.at[s, slot],
            device_id=(peer, tp), device_id_type=MESH,
        )

    def push(s, slot, which, peer, src=None):
        copy = copy_of(s, slot, which, peer, src)
        copy.start()
        sends.append(copy)

    def own(s):
        src = None
        if Q0 <= s < O0:
            src = wq_ref.at[pl.ds(steps[s][2], CHUNK)]
        elif O0 <= s < KV:
            src = wo_ref.at[pl.ds(steps[s][2], CHUNK)]
        push(s, me, 3, x_peer, src)
        for k in (0, 2, 1):
            push(s, me, k, z_peers[k], src)
        push(s, me, 4, c_peer, src)

    def from_z(s):
        for k in (2, 0, 1):
            slot = z_peers[k]
            copy_of(s, slot, 0, x_peer).wait_recv()
            push(s, slot, 5 + k, x_peer)
            push(s, slot, 8 + k, c_peer)

    def from_x(s):
        for k in range(4):
            slot = index(lax.rem(z + k, 4), 1 - x, c)
            copy_of(s, slot, 0, x_peer).wait_recv()
            push(s, slot, 11 + k, c_peer)

    def from_c(s):
        for k in range(4):
            for xx in range(2):
                slot = index(lax.rem(z + k, 4), xx, 1 - c)
                copy_of(s, slot, 0, c_peer).wait_recv()

    own(0)
    own(1)
    own(Q0)
    own(Q0 + 1)

    tok_copy.wait_recv()
    lower = tok[0].astype(jnp.float32)
    upper = tok[1].astype(jnp.float32)
    square = jnp.sum(lower * lower, axis=1, keepdims=True) + jnp.sum(upper * upper, axis=1, keepdims=True)
    scale = lax.rsqrt(square / (2 * width) + 1e-06)
    gain = gain_ref[...].astype(jnp.float32)
    normed[:, :width] = (lower * scale * gain[:, :width]).astype(jnp.bfloat16)
    normed[:, width:] = (upper * scale * gain[:, width:]).astype(jnp.bfloat16)

    from_z(0)
    own(Q0 + 2)
    from_z(1)
    from_x(0)
    from_z(Q0)
    from_x(1)
    own(Q0 + 3)
    from_c(0)

    mine_seg = segcol_ref[...]
    below = jnp.zeros((rows, rows), jnp.float32)
    for slot in range(16):
        below = below + (seg[slot] < mine_seg).astype(jnp.float32)
    start = jnp.sum(below, axis=1, keepdims=True)
    token_index = me * rows + lax.broadcasted_iota(jnp.int32, (rows, 1), 0)
    angle = (token_index.astype(jnp.float32) - start) * freq_ref[...]
    cosine = jnp.cos(angle)
    sine = jnp.sin(angle)
    lane = lax.broadcasted_iota(jnp.int32, angle.shape, 1)
    sine = jnp.where(lane < HD // 4, -sine, sine)

    def turn(part, cosine, sine):
        return part * cosine + pltpu.roll(part, HD // 4, 1) * sine

    from_z(Q0 + 1)
    from_x(Q0)
    own(Q0 + 4)
    from_c(1)
    raw = jnp.dot(normed[...], wkv[...], preferred_element_type=jnp.float32)
    first = jnp.where(tp == 0, turn(raw[:, : HD // 2], cosine, sine), raw[:, : HD // 2])
    half[pl.ds(tp, 1), :, : HD // 2] = first.astype(jnp.bfloat16)[None]
    half[pl.ds(tp, 1), :, HD // 2 :] = raw[:, HD // 2 :].astype(jnp.bfloat16)[None]
    half_copy = pair(1, half.at[tp], half.at[tp])
    half_copy.start()
    from_z(Q0 + 2)
    from_x(Q0 + 1)
    half_copy.wait_recv()
    own_rows = pl.ds(pl.multiple_of(me * rows, rows), rows)
    kv[own_rows, :HD] = half[0]
    kv[own_rows, HD:] = half[1]
    cache_ref[:, :HD] = half[0]
    cache_ref[:, HD:] = half[1]
    own(KV)
    own(O0)
    from_z(Q0 + 3)
    from_x(Q0 + 2)
    own(O0 + 1)
    from_z(Q0 + 4)
    from_x(Q0 + 3)
    from_z(KV)
    own(O0 + 2)
    from_x(Q0 + 4)
    from_z(O0)
    from_x(KV)
    for copy in mine:
        copy.wait()
    for at in range(per):
        from_c(Q0 + at)

    for head in range(heads):
        raw = jnp.dot(normed[...], wq[:, head * HD : (head + 1) * HD], preferred_element_type=jnp.float32)
        queries[:, head * HD : head * HD + HD // 2] = turn(raw[:, : HD // 2], cosine, sine).astype(jnp.bfloat16)
        queries[:, head * HD + HD // 2 : (head + 1) * HD] = raw[:, HD // 2 :].astype(jnp.bfloat16)

    own(O0 + 3)
    from_z(O0 + 1)
    from_x(O0)
    from_c(KV)

    def attend(head):
        scores = lax.dot_general(
            queries[:, head * HD : (head + 1) * HD], kv[:, :HD],
            (((1,), (1,)), ((), ())), preferred_element_type=jnp.float32,
        ) * HD ** (-0.5)
        key_seg = jnp.concatenate([seg[slot] for slot in range(16)], axis=1)
        key_index = lax.broadcasted_iota(jnp.int32, (1, total), 1)
        live = (key_seg == mine_seg) & (key_index <= token_index) & (token_index - key_index < WINDOW)
        scores = jnp.where(live, scores, -1e30)
        peak = jnp.max(scores, axis=1, keepdims=True)
        powered = jnp.exp(scores - peak)
        weights = (powered / jnp.sum(powered, axis=1, keepdims=True)).astype(jnp.bfloat16)
        attended[:, head * HD : (head + 1) * HD] = jnp.dot(
            weights, kv[:, HD:], preferred_element_type=jnp.float32
        ).astype(jnp.bfloat16)

    for at in range(max(heads, per)):
        if at < heads:
            attend(at)
        if 4 + at < per:
            own(O0 + 4 + at)
        if 2 + at < per:
            from_z(O0 + 2 + at)
        if 1 + at < per:
            from_x(O0 + 1 + at)
    for at in range(per):
        from_c(O0 + at)

    def project(which):
        rows_of = pl.ds(pl.multiple_of(which * width, 256), width)
        return lax.dot_general(
            attended[...], wo[rows_of, :], (((1,), (1,)), ((), ())), preferred_element_type=jnp.float32
        ).astype(jnp.bfloat16)

    partial[...] = project(1 - tp)
    out_copy = pair(2, partial, other)
    out_copy.start()
    own_part = project(tp).astype(jnp.float32)
    out_copy.wait_recv()
    summed = own_part + other[...].astype(jnp.float32)
    hidden_ref[...] = (tok_ref[...].astype(jnp.float32) + summed).astype(jnp.bfloat16)

    for copy in sends + [tok_copy, half_copy, out_copy]:
        copy.wait_send()


def per_device_kernel(tokens, seg_ids, norm_gain, w_query, w_keyval, w_out):
    rows, width = tokens.shape
    shard, count = w_query.shape
    model = shard * 16
    quarter = HD // 4
    freq = 10000.0 ** (-jnp.arange(quarter, dtype=jnp.float32) / quarter)
    freq = jnp.concatenate([freq, freq]).reshape(1, 2 * quarter)
    steps = 3 + 2 * (shard // CHUNK)
    vmem = pl.BlockSpec(memory_space=pltpu.VMEM)
    bf16 = jnp.bfloat16
    return pl.pallas_call(
        block_kernel,
        out_shape=(
            jax.ShapeDtypeStruct((rows, width), bf16),
            jax.ShapeDtypeStruct((rows, 2 * HD), bf16),
        ),
        in_specs=[vmem] * 8,
        out_specs=(vmem, vmem),
        scratch_shapes=[
            pltpu.VMEM((2, rows, width), bf16),
            pltpu.VMEM((rows, model), bf16),
            pltpu.VMEM((16, 1, rows), jnp.int32),
            pltpu.VMEM((model, HD), bf16),
            pltpu.VMEM((model, count), bf16),
            pltpu.VMEM((model, count), bf16),
            pltpu.VMEM((16 * rows, 2 * HD), bf16),
            pltpu.VMEM((2, rows, HD), bf16),
            pltpu.VMEM((rows, count), bf16),
            pltpu.VMEM((rows, count), bf16),
            pltpu.VMEM((rows, width), bf16),
            pltpu.VMEM((rows, width), bf16),
            pltpu.SemaphoreType.DMA((2,)),
            pltpu.SemaphoreType.DMA((steps, 15)),
            pltpu.SemaphoreType.DMA((steps, 16)),
            pltpu.SemaphoreType.DMA((3,)),
            pltpu.SemaphoreType.DMA((3,)),
        ],
        compiler_params=pltpu.CompilerParams(
            collective_id=0, has_side_effects=True, vmem_limit_bytes=48 * 1024 * 1024
        ),
    )(
        tokens, seg_ids.reshape(1, rows), seg_ids.reshape(rows, 1), norm_gain.reshape(1, model), freq,
        w_query, w_keyval, w_out.T,
    )


def solution(mesh):
    in_specs = (P("seq", "tp"), P("seq"), P(), P("seq", "tp"), P("seq", None), P("tp", "seq"))
    out_specs = (P("seq", "tp"), P("seq", None))
    fits = mesh.shape["seq"] == 16 and mesh.shape["tp"] == 2
    return jax.shard_map(
        per_device_kernel if fits else per_device,
        mesh=mesh, in_specs=in_specs, out_specs=out_specs, check_vma=False,
    )
```

```python
import jax
import jax.numpy as jnp
from jax import lax
from jax.experimental import pallas as pl
from jax.experimental.pallas import tpu as pltpu
from jax.sharding import PartitionSpec as P

HD = 256
WINDOW = 2048
SEG_MEAN = 512
CHUNK = 32
ACROSS = 99


def from_behind(x, axis, by):
    devices = lax.axis_size(axis)
    pairs = [(i, i + by) for i in range(devices) if 0 <= i + by < devices]
    return lax.ppermute(x, axis, pairs)


def rms_norm(values, gain):
    wide = values.astype(jnp.float32)
    scaled = wide * lax.rsqrt(jnp.mean(wide * wide, axis=-1, keepdims=True) + 1e-06)
    return (scaled * gain.astype(jnp.float32)).astype(jnp.bfloat16)


def rotate(tensor, positions):
    quarter = tensor.shape[-1] // 4
    freq = 10000.0 ** (-jnp.arange(quarter, dtype=jnp.float32) / quarter)
    angle = positions[:, None, None] * freq
    cosine = jnp.cos(angle)
    sine = jnp.sin(angle)
    first = tensor[..., :quarter]
    second = tensor[..., quarter : 2 * quarter]
    return jnp.concatenate(
        [
            first * cosine - second * sine,
            second * cosine + first * sine,
            tensor[..., 2 * quarter :],
        ],
        axis=-1,
    )


def per_device(tokens, seg_ids, norm_gain, w_query, w_keyval, w_out):
    tok_rows = tokens.shape[0]
    seq_count = lax.axis_size("seq")
    my_index = lax.axis_index("seq")
    gathered = lax.all_gather(tokens, "tp", axis=1, tiled=True)
    normed = rms_norm(gathered, norm_gain)
    seg_total = tok_rows * seq_count // SEG_MEAN
    labels = jnp.arange(seg_total, dtype=jnp.int32)
    below = jnp.sum((seg_ids[None, :] < labels[:, None]).astype(jnp.int32), axis=1)
    starts = lax.psum(below, "seq")
    own_start = jnp.sum(jnp.where(seg_ids[:, None] == labels[None, :], starts[None, :], 0), axis=1)
    token_index = my_index * tok_rows + jnp.arange(tok_rows, dtype=jnp.int32)
    positions = (token_index - own_start).astype(jnp.float32)
    query_raw = jnp.dot(
        normed,
        lax.all_gather(w_query, "seq", axis=0, tiled=True),
        preferred_element_type=jnp.float32,
    )
    keyval_raw = jnp.dot(
        normed,
        lax.all_gather(w_keyval, "seq", axis=0, tiled=True),
        preferred_element_type=jnp.float32,
    )
    local_heads = w_query.shape[1] // HD
    queries = rotate(query_raw.reshape(tok_rows, local_heads, HD), positions).astype(jnp.bfloat16)
    key_rows = rotate(keyval_raw[:, None, :HD], positions)[:, 0, :]
    kv_cache = jnp.concatenate([key_rows, keyval_raw[:, HD:]], axis=1).astype(jnp.bfloat16)
    reach = min(WINDOW // tok_rows, seq_count - 1)

    def advance(counter, state):
        current, current_seg, store, store_seg = state
        current, current_seg = from_behind((current, current_seg), "seq", 1)
        slot = reach - 1 - counter
        store = lax.dynamic_update_slice_in_dim(store, current[None], slot, 0)
        store_seg = lax.dynamic_update_slice_in_dim(store_seg, current_seg[None], slot, 0)
        return (current, current_seg, store, store_seg)

    if reach == seq_count - 1:
        block_kv = lax.all_gather(kv_cache, "seq", axis=0, tiled=True)
        block_seg = lax.all_gather(seg_ids, "seq", axis=0, tiled=True)
        first_key = 0
    else:
        store_init = jnp.zeros((reach, tok_rows, kv_cache.shape[1]), jnp.bfloat16)
        seg_init = jnp.zeros((reach, tok_rows), jnp.int32)
        final_state = lax.fori_loop(0, reach, advance, (kv_cache, seg_ids, store_init, seg_init))
        block_kv = jnp.concatenate(
            [final_state[2].reshape(reach * tok_rows, kv_cache.shape[1]), kv_cache], axis=0
        )
        block_seg = jnp.concatenate([final_state[3].reshape(reach * tok_rows), seg_ids], axis=0)
        first_key = (my_index - reach) * tok_rows
    key_index = first_key + jnp.arange((reach + 1) * tok_rows, dtype=jnp.int32)
    live = (block_seg[None, :] == seg_ids[:, None]) & (key_index[None, :] <= token_index[:, None])
    live = live & (token_index[:, None] - key_index[None, :] < WINDOW) & (key_index[None, :] >= 0)
    all_keys = block_kv[:, :HD]
    all_values = block_kv[:, HD:]
    head_outputs = []
    for head_idx in range(local_heads):
        scores = lax.dot_general(
            queries[:, head_idx, :],
            all_keys,
            (((1,), (1,)), ((), ())),
            preferred_element_type=jnp.float32,
        ) * HD ** (-0.5)
        scores = jnp.where(live, scores, -1e30)
        peak = jnp.max(scores, axis=1, keepdims=True)
        powered = jnp.exp(scores - peak)
        weights = (powered / jnp.sum(powered, axis=1, keepdims=True)).astype(jnp.bfloat16)
        head_outputs.append(
            jnp.dot(weights, all_values, preferred_element_type=jnp.float32).astype(jnp.bfloat16)
        )
    attended = jnp.concatenate(head_outputs, axis=1)
    partial_value = jnp.dot(
        attended,
        lax.all_gather(w_out, "seq", axis=1, tiled=True),
        preferred_element_type=jnp.float32,
    )
    summed = lax.psum_scatter(
        partial_value.astype(jnp.bfloat16), "tp", scatter_dimension=1, tiled=True
    ).astype(jnp.float32)
    hidden = (tokens.astype(jnp.float32) + summed).astype(jnp.bfloat16)
    return (hidden, kv_cache)


MESH = pl.DeviceIdType.MESH


def block_kernel(
    tok_ref, seg_ref, segcol_ref, gain_ref, freq_ref, wq_ref, wkv_ref, wo_ref,
    hidden_ref, cache_ref,
    tok, normed, seg, wkv, wq, wo, kv, queries, attended, partial, other,
    local_sem, send_sem, recv_sem, pair_send, pair_recv,
):
    me = lax.axis_index("seq")
    tp = lax.axis_index("tp")
    z, x, c = me // 4, lax.rem(me // 2, 2), lax.rem(me, 2)
    rows = tok_ref.shape[0]
    width = tok_ref.shape[1]
    shard = wq_ref.shape[0]
    count = wq_ref.shape[1]
    heads = count // HD
    total = rows * 16

    def index(zz, xx, cc):
        return (zz * 2 + xx) * 2 + cc

    z_peers = [index(lax.rem(z + k, 4), x, c) for k in (1, 2, 3)]
    low = z - 1 + 2 * (1 - (z + 3) // 4)
    far = 3 * (1 - z // 2)
    origins = (low, 6 - z - low - far, far)
    x_peer = index(z, 1 - x, c)
    c_peer = index(z, x, 1 - c)

    barrier = pltpu.get_barrier_semaphore()
    for peer in z_peers + [x_peer, c_peer]:
        pl.semaphore_signal(barrier, inc=1, device_id=(peer, tp), device_id_type=MESH)
    pl.semaphore_signal(barrier, inc=1, device_id=(me, 1 - tp), device_id_type=MESH)

    mine = [
        pltpu.make_async_copy(wq_ref, wq.at[pl.ds(pl.multiple_of(me * shard, shard), shard)], local_sem.at[0]),
        pltpu.make_async_copy(wo_ref, wo.at[pl.ds(pl.multiple_of(me * shard, shard), shard)], local_sem.at[1]),
    ]
    for copy in mine:
        copy.start()
    wkv[pl.ds(pl.multiple_of(me * shard, shard), shard), :] = jnp.where(
        tp == 0, wkv_ref[:, :HD], wkv_ref[:, HD:]
    )
    seg[me] = seg_ref[...]
    pl.semaphore_wait(barrier, 6)

    def pair(which, src, dst):
        return pltpu.make_async_remote_copy(
            src_ref=src, dst_ref=dst, send_sem=pair_send.at[which], recv_sem=pair_recv.at[which],
            device_id=(me, 1 - tp), device_id_type=MESH,
        )

    tok_copy = pair(0, tok_ref, tok.at[tp])
    tok_copy.start()
    tok[pl.ds(tp, 1)] = tok_ref[...][None]

    steps = [(seg, 0, 0, 0), (wkv, shard, 0, shard)]
    steps += [(wq, shard, at, CHUNK) for at in range(0, shard, CHUNK)]
    steps += [(wo, shard, at, CHUNK) for at in range(0, shard, CHUNK)]
    steps += [(kv.at[tp], rows, 0, rows), (kv.at[1 - tp], rows, 0, rows)]
    per = shard // CHUNK
    Q0, O0, KV, KY = 2, 2 + per, 2 + 2 * per, 3 + 2 * per
    across = (Q0 + ACROSS, O0 + ACROSS)
    used = [0] * len(steps)
    sends = []

    def view(s, slot):
        buffer, each, at, size = steps[s]
        if each == 0:
            return buffer.at[slot]
        return buffer.at[pl.ds(pl.multiple_of(slot * each + at, 16), size)]

    def arrived(s, slot):
        pltpu.make_async_remote_copy(
            src_ref=view(s, slot), dst_ref=view(s, slot),
            send_sem=send_sem.at[s, 0], recv_sem=recv_sem.at[s, slot],
            device_id=(x_peer, tp), device_id_type=MESH,
        ).wait_recv()

    def push(s, slot, peer, src=None, when=None, land=None, plane=None):
        which = used[s]
        used[s] += 1
        copy = pltpu.make_async_remote_copy(
            src_ref=view(s, slot) if src is None else src, dst_ref=view(s, slot),
            send_sem=send_sem.at[s, which], recv_sem=recv_sem.at[s if land is None else land, slot],
            device_id=(peer, tp if plane is None else plane), device_id_type=MESH,
        )
        if when is None:
            copy.start()
        else:
            pl.when(when)(copy.start)
        sends.append((copy, when))

    up, down = me + 4, me - 4

    def both_ways(s, slot, src=None):
        push(s, slot, up, src, when=z < 3)
        push(s, slot, down, src, when=z > 0)

    def onward(s, slot, origin):
        push(s, slot, up, when=(origin < z) & (z < 3))
        push(s, slot, down, when=(origin > z) & (z > 0))

    def to_plane(s, slot):
        if s == KV:
            push(s, slot, me, land=KY, plane=1 - tp)

    def own(s):
        src = None
        if Q0 <= s < O0:
            src = wq_ref.at[pl.ds(steps[s][2], CHUNK)]
        elif O0 <= s < KV:
            src = wo_ref.at[pl.ds(steps[s][2], CHUNK)]
        to_plane(s, me)
        push(s, me, x_peer, src)
        both_ways(s, me, src)
        push(s, me, c_peer, src)
        if s in across:
            slot = index(z, 1 - x, c)
            late.append((s, slot))

    late = []

    def turn_late():
        while late:
            s, slot = late.pop(0)
            arrived(s, slot)
            both_ways(s, slot)
            push(s, slot, c_peer)

    def from_z(s):
        turn_late()
        for origin in origins:
            slot = index(origin, x, c)
            arrived(s, slot)
            onward(s, slot, origin)
            if s not in across:
                push(s, slot, x_peer)
            to_plane(s, slot)
            push(s, slot, c_peer)
            if s in across:
                slot = index(origin, 1 - x, c)
                arrived(s, slot)
                onward(s, slot, origin)
                push(s, slot, c_peer)

    def from_x(s):
        if s in across:
            return
        for k in range(4):
            slot = index(lax.rem(z + k, 4), 1 - x, c)
            arrived(s, slot)
            to_plane(s, slot)
            push(s, slot, c_peer)

    def from_y():
        for k in range(4):
            for k2 in range(2):
                slot = index(lax.rem(z + k, 4), lax.rem(x + k2, 2), c)
                arrived(KY, slot)
                push(KY, slot, c_peer)

    def from_c(s):
        for k in range(4):
            for xx in range(2):
                arrived(s, index(lax.rem(z + k, 4), xx, 1 - c))

    own(0)
    own(1)
    for at in range(per):
        own(Q0 + at)

    tok_copy.wait_recv()
    lower = tok[0].astype(jnp.float32)
    upper = tok[1].astype(jnp.float32)
    square = jnp.sum(lower * lower, axis=1, keepdims=True) + jnp.sum(upper * upper, axis=1, keepdims=True)
    scale = lax.rsqrt(square / (2 * width) + 1e-06)
    gain = gain_ref[...].astype(jnp.float32)
    normed[:, :width] = (lower * scale * gain[:, :width]).astype(jnp.bfloat16)
    normed[:, width:] = (upper * scale * gain[:, width:]).astype(jnp.bfloat16)

    from_z(0)
    from_z(1)
    from_x(0)
    from_z(Q0)
    from_x(1)
    from_c(0)

    mine_seg = segcol_ref[...]
    below = jnp.zeros((rows, rows), jnp.float32)
    for slot in range(16):
        below = below + (seg[slot] < mine_seg).astype(jnp.float32)
    start = jnp.sum(below, axis=1, keepdims=True)
    token_index = me * rows + lax.broadcasted_iota(jnp.int32, (rows, 1), 0)
    angle = (token_index.astype(jnp.float32) - start) * freq_ref[...]
    cosine = jnp.cos(angle)
    sine = jnp.sin(angle)
    lane = lax.broadcasted_iota(jnp.int32, angle.shape, 1)
    sine = jnp.where(lane < HD // 4, -sine, sine)

    def turn(part, cosine, sine):
        return part * cosine + pltpu.roll(part, HD // 4, 1) * sine

    from_z(Q0 + 1)
    from_x(Q0)
    from_c(1)
    raw = jnp.dot(normed[...], wkv[...], preferred_element_type=jnp.float32)
    first = jnp.where(tp == 0, turn(raw[:, : HD // 2], cosine, sine), raw[:, : HD // 2])
    own_rows = pl.ds(pl.multiple_of(me * rows, rows), rows)
    kv[pl.ds(tp, 1), own_rows, : HD // 2] = first.astype(jnp.bfloat16)[None]
    kv[pl.ds(tp, 1), own_rows, HD // 2 :] = raw[:, HD // 2 :].astype(jnp.bfloat16)[None]
    own(KV)
    own(O0)
    from_z(Q0 + 2)
    from_x(Q0 + 1)
    own(O0 + 1)
    from_z(Q0 + 3)
    from_x(Q0 + 2)
    own(O0 + 2)
    from_z(Q0 + 4)
    from_x(Q0 + 3)
    own(O0 + 3)
    from_z(KV)
    from_x(Q0 + 4)
    own(O0 + 4)
    from_z(O0)
    from_x(KV)
    for copy in mine:
        copy.wait()
    for at in range(per):
        from_c(Q0 + at)

    for head in range(heads):
        raw = jnp.dot(normed[...], wq[:, head * HD : (head + 1) * HD], preferred_element_type=jnp.float32)
        queries[:, head * HD : head * HD + HD // 2] = turn(raw[:, : HD // 2], cosine, sine).astype(jnp.bfloat16)
        queries[:, head * HD + HD // 2 : (head + 1) * HD] = raw[:, HD // 2 :].astype(jnp.bfloat16)

    from_z(O0 + 1)
    from_x(O0)
    from_y()
    from_z(O0 + 2)
    from_x(O0 + 1)
    from_c(KV)
    from_c(KY)
    cache_ref[:, :HD] = kv[0, own_rows, :]
    cache_ref[:, HD:] = kv[1, own_rows, :]

    def attend(head):
        scores = lax.dot_general(
            queries[:, head * HD : (head + 1) * HD], kv[0],
            (((1,), (1,)), ((), ())), preferred_element_type=jnp.float32,
        ) * HD ** (-0.5)
        key_seg = jnp.concatenate([seg[slot] for slot in range(16)], axis=1)
        key_index = lax.broadcasted_iota(jnp.int32, (1, total), 1)
        live = (key_seg == mine_seg) & (key_index <= token_index) & (token_index - key_index < WINDOW)
        scores = jnp.where(live, scores, -1e30)
        peak = jnp.max(scores, axis=1, keepdims=True)
        powered = jnp.exp(scores - peak)
        weights = (powered / jnp.sum(powered, axis=1, keepdims=True)).astype(jnp.bfloat16)
        attended[:, head * HD : (head + 1) * HD] = jnp.dot(
            weights, kv[1], preferred_element_type=jnp.float32
        ).astype(jnp.bfloat16)

    for at in range(max(heads, per)):
        if at < heads:
            attend(at)
        if 3 + at < per:
            from_z(O0 + 3 + at)
        if 2 + at < per:
            from_x(O0 + 2 + at)
    for at in range(per):
        from_c(O0 + at)

    def project(which):
        rows_of = pl.ds(pl.multiple_of(which * width, 256), width)
        return lax.dot_general(
            attended[...], wo[rows_of, :], (((1,), (1,)), ((), ())), preferred_element_type=jnp.float32
        ).astype(jnp.bfloat16)

    partial[...] = project(1 - tp)
    out_copy = pair(1, partial, other)
    out_copy.start()
    own_part = project(tp).astype(jnp.float32)
    out_copy.wait_recv()
    summed = own_part + other[...].astype(jnp.float32)
    hidden_ref[...] = (tok_ref[...].astype(jnp.float32) + summed).astype(jnp.bfloat16)

    for copy in [tok_copy, out_copy]:
        copy.wait_send()
    for copy, when in sends:
        if when is None:
            copy.wait_send()
        else:
            pl.when(when)(copy.wait_send)


def per_device_kernel(tokens, seg_ids, norm_gain, w_query, w_keyval, w_out):
    rows, width = tokens.shape
    shard, count = w_query.shape
    model = shard * 16
    quarter = HD // 4
    freq = 10000.0 ** (-jnp.arange(quarter, dtype=jnp.float32) / quarter)
    freq = jnp.concatenate([freq, freq]).reshape(1, 2 * quarter)
    steps = 4 + 2 * (shard // CHUNK)
    vmem = pl.BlockSpec(memory_space=pltpu.VMEM)
    bf16 = jnp.bfloat16
    return pl.pallas_call(
        block_kernel,
        out_shape=(
            jax.ShapeDtypeStruct((rows, width), bf16),
            jax.ShapeDtypeStruct((rows, 2 * HD), bf16),
        ),
        in_specs=[vmem] * 8,
        out_specs=(vmem, vmem),
        scratch_shapes=[
            pltpu.VMEM((2, rows, width), bf16),
            pltpu.VMEM((rows, model), bf16),
            pltpu.VMEM((16, 1, rows), jnp.int32),
            pltpu.VMEM((model, HD), bf16),
            pltpu.VMEM((model, count), bf16),
            pltpu.VMEM((model, count), bf16),
            pltpu.VMEM((2, 16 * rows, HD), bf16),
            pltpu.VMEM((rows, count), bf16),
            pltpu.VMEM((rows, count), bf16),
            pltpu.VMEM((rows, width), bf16),
            pltpu.VMEM((rows, width), bf16),
            pltpu.SemaphoreType.DMA((2,)),
            pltpu.SemaphoreType.DMA((steps, 32)),
            pltpu.SemaphoreType.DMA((steps, 16)),
            pltpu.SemaphoreType.DMA((2,)),
            pltpu.SemaphoreType.DMA((2,)),
        ],
        compiler_params=pltpu.CompilerParams(
            collective_id=0, has_side_effects=True, vmem_limit_bytes=48 * 1024 * 1024
        ),
    )(
        tokens, seg_ids.reshape(1, rows), seg_ids.reshape(rows, 1), norm_gain.reshape(1, model), freq,
        w_query, w_keyval, w_out.T,
    )


def solution(mesh):
    in_specs = (P("seq", "tp"), P("seq"), P(), P("seq", "tp"), P("seq", None), P("tp", "seq"))
    out_specs = (P("seq", "tp"), P("seq", None))
    fits = mesh.shape["seq"] == 16 and mesh.shape["tp"] == 2
    return jax.shard_map(
        per_device_kernel if fits else per_device,
        mesh=mesh, in_specs=in_specs, out_specs=out_specs, check_vma=False,
    )
```
